32 devices in a mesh: parts: 2 (over x), node: 2 (over core), dev: 8 (over z, y).
Axes of the slice: x: 2, y: 2, z: 4, core: 2. Of those that a mesh axis runs over, the one named last changes fastest.
Arguments:
- tokens: bfloat16 [512, 7168], P(('parts', 'node', 'dev')), parts along dimension 0, may hold values from -6 to 6
- routes: int32 [512, 2], P(('parts', 'node', 'dev')), parts along dimension 0, may hold values from 0 to 3, all different within a row; in each aligned block of 16 rows (0 to 15, 16 to 31, ...) at most 16 rows name the same one
- route_weight: float32 [512, 2], P(('parts', 'node', 'dev')), parts along dimension 0, may hold values from 0.1 to 1
- w_gate: bfloat16 [16, 7168, 256], P(('node', 'dev')), may hold values from -0.0625 to 0.0625
- w_up: bfloat16 [16, 7168, 256], P(('node', 'dev')), may hold values from -0.0625 to 0.0625
- w_down: bfloat16 [16, 256, 7168], P(('node', 'dev')), may hold values from -0.1875 to 0.1875
- queries: bfloat16 [32, 128, 576], P(('parts', 'node', 'dev')), parts along dimension 0, may hold values from -2000 to 2000
- latent_cache: bfloat16 [32, 1024, 576], P(('parts', 'node', 'dev')), parts along dimension 0, may hold values from -8 to 8
- lengths: int32 [32], P(('parts', 'node', 'dev')), parts along dimension 0, may hold values from 128 to 1024, as said below
Outputs:
- moe_out: bfloat16 [512, 7168], P(('parts', 'node', 'dev')), parts along dimension 0
- context: bfloat16 [32, 128, 512], P(('parts', 'node', 'dev')), parts along dimension 0
The draws below stay inside these ranges and needn't reach their ends.
There are 2 independent parts, one for each index of `parts`. The reference program is written for one: setup_inputs(seed, part) draws one part's arguments, and reference() takes and returns one part's arrays. A program takes and returns all parts, laid end to end along the dimension named above; an argument that names none is the same for every part. Nothing has to cross between parts.
Inputs may be any that keep to these rules, and one draw needn't show every extreme that they name: `routes`: each token names 2 different experts; the tokens of one device name no expert more than 16 times, a bound that some block reaches. `lengths`: some row of every part has length 1024.
All inputs are finite; a program needn't handle non-finite values.
Results may differ from the reference program's by a relative error of at most 0.0058.
Values may be sent and summed in bfloat16 or wider, within the bound.
No kernel may reach another device: no remote copies, remote signals or barrier semaphores. Data moves between devices by JAX's collectives and lax.ppermute only.
A program may use at most 128 MiB of HBM per device.

```python
import math
import jax
import jax.numpy as jnp
import numpy as np
from jax import lax

D = 7168
HEADS = 128
LAT = 512
ROPE = 64
HEAD_QK = 192
SLICES = 4
HID_DEV = 256
TOK = 16
LEN = 1024
EXP_HIDDEN = 1024
EXPERTS = 4
TOP = 2
CAP = 16
TOKENS = 256
AROWS_ALL = 16
N_NODE = 2
N_DEV = 8


def cache_base(key):
    values = jax.random.normal(key, (AROWS_ALL, LEN, LAT + ROPE), jnp.float32)
    rope_second = values[:, 2, LAT:]
    return values.at[:, 2, LAT:].set(rope_second)


def draw_latent_cache(key, part):
    values = cache_base(key)
    return values.astype(jnp.bfloat16)


def draw_queries(key, part):
    key = jax.random.fold_in(key, 7)
    values = jax.random.normal(key, (AROWS_ALL, HEADS, LAT + ROPE), jnp.float32)
    return values.astype(jnp.bfloat16)


def draw_lengths(key, part):
    key = jax.random.fold_in(key, 11)
    drawn = jax.random.randint(key, (AROWS_ALL,), LEN // 8, LEN + 1, dtype=jnp.int32)
    return drawn.at[0].set(LEN)


def steps_of(rng, dims, shards, smallest, top_value):
    level, own = 1.0, jax.random.fold_in(rng, 6)
    for dim, blocks in shards:
        heights = jnp.exp(jax.random.uniform(jax.random.fold_in(own, dim), (blocks,), jnp.float32, smallest / len(shards), top_value / len(shards)))
        level = level * jnp.repeat(heights, dims[dim] // blocks).reshape([-1 if axis == dim else 1 for axis in range(len(dims))])
    return level


def assign_block(rng, own, number, rows, number_of, top, most, slope):
    order = jax.random.permutation(rng, number_of)
    heavy_load, usual = portions_of(number_of, rows * top, most, slope, True), portions_of(number_of, rows * top, most, slope, False)
    places = jnp.arange(number_of)

    def named(sizes, offset_by):
        used = int((sizes > 0).sum())
        fixed = max(1, used // 4)
        shifted = fixed + (places - fixed + offset_by * (used - fixed)) % max(1, number_of - fixed)
        return jnp.zeros((number_of,), jnp.int32).at[order[jnp.where(places < fixed, places, shifted)]].set(jnp.asarray(sizes, jnp.int32))

    sizes = jnp.where(number % 4 == 0, named(heavy_load, number // 4), named(usual, number - number // 4 - 1))
    mixed = jax.random.permutation(jax.random.fold_in(own, 3), number_of)
    source_of, receiver = mixed[0:number_of // 2 * 2:2], mixed[1:number_of // 2 * 2:2]
    margin = jnp.minimum(sizes[source_of] - 1, most - sizes[receiver]) // 2
    margin = jnp.where((source_of == order[0]) | (receiver == order[0]) | (sizes[receiver] == 0), 0, jnp.maximum(margin, 0))
    shifted = jax.random.randint(jax.random.fold_in(own, 4), (number_of // 2,), 0, 1 << 20) % (margin + 1)
    sizes = sizes.at[source_of].add(-shifted).at[receiver].add(shifted)
    items = jnp.searchsorted(jnp.cumsum(sizes), jnp.arange(rows * top), side="right").astype(jnp.int32)
    grid = items.reshape(top, rows).T
    grid = grid[jax.random.permutation(jax.random.fold_in(own, 1), rows)]
    offset_by = jax.random.randint(jax.random.fold_in(own, 2), (rows, 1), 0, top)
    return jnp.take_along_axis(grid, (jnp.arange(top)[None, :] + offset_by) % top, axis=1)


def portions_of(amount, total, limit, lean, full):
    weights = [(1 << 20) // math.isqrt(rank ** lean) + 1 for rank in range(1, amount + 1)]
    largest = limit if full else min(limit, max(-(-total // amount), total * weights[0] // sum(weights)))
    least = 1 if total - largest >= amount - 1 else 0
    holding, rest = [largest] + [least] * (amount - 1), total - largest - least * (amount - 1)
    while rest > 0:
        candidates = [i for i in range(1, amount) if holding[i] < largest] or [i for i in range(1, amount) if holding[i] < limit]
        pool, budget = sum([weights[i] for i in candidates]), rest
        for i in candidates:
            more = min(limit - holding[i], max(1, budget * weights[i] // pool), rest)
            holding[i] = holding[i] + more
            rest = rest - more
    return np.array(holding)


def scatter_about(rng, shape, deviation, limit, split=(), held_as=jnp.bfloat16):
    values = deviation * jax.random.normal(rng, shape, jnp.float32)
    if split:
        values = values * steps_of(rng, shape, split, -0.22, 0.18)
    return jnp.clip(values, -limit, limit).astype(held_as)


def setup_inputs(seed: int = 0, part: int = 0) -> dict:
    arg_keys = jax.random.split(jax.random.key(seed), 10)
    part_splits = jax.random.split(jax.random.fold_in(arg_keys[9], part), 10)
    tokens = scatter_about(part_splits[0], (TOKENS, D), 1.0, 6.0, ((0, 16),))
    routes_keys = jax.random.split(jax.random.fold_in(part_splits[1], 1), TOKENS // TOK)
    routes_turns = jax.random.permutation(jax.random.fold_in(part_splits[1], 3), TOKENS // TOK)
    routes = jax.vmap(lambda own, number: assign_block(jax.random.fold_in(part_splits[1], 2), own, number, TOK, EXPERTS, TOP, CAP, 2))(routes_keys, routes_turns).reshape((TOKENS, TOP))
    route_weight = jnp.clip(jnp.exp(math.log(1.0) - 2.3025851 * jax.random.uniform(part_splits[2], (TOKENS, TOP), jnp.float32) ** steps_of(part_splits[2], (TOKENS, TOP), ((0, 16),), -0.2, 0.2)), 0.1, 1.0)
    w_gate = scatter_about(arg_keys[3], (EXPERTS * SLICES, D, HID_DEV), D ** -0.5, 0.0625, ((0, 16),))
    w_up = scatter_about(arg_keys[4], (EXPERTS * SLICES, D, HID_DEV), D ** -0.5, 0.0625, ((0, 16),))
    w_down = scatter_about(arg_keys[5], (EXPERTS * SLICES, HID_DEV, D), EXP_HIDDEN ** -0.5, 0.1875, ((0, 16),))
    queries = draw_queries(jax.random.fold_in(jax.random.fold_in(arg_keys[9], part), 71), part)
    latent_cache = draw_latent_cache(jax.random.fold_in(jax.random.fold_in(arg_keys[9], part), 71), part)
    lengths = draw_lengths(jax.random.fold_in(jax.random.fold_in(arg_keys[9], part), 71), part)
    return dict(tokens=tokens, routes=routes, route_weight=route_weight, w_gate=w_gate, w_up=w_up, w_down=w_down, queries=queries, latent_cache=latent_cache, lengths=lengths)


def slot_tables(routes, route_weight, experts_all, capacity):
    choices_hit = routes[:, :, None] == jnp.arange(experts_all, dtype=jnp.int32)[None, None, :]
    member = jnp.sum(choices_hit.astype(jnp.int32), axis=1)
    combine = jnp.sum(jnp.where(choices_hit, route_weight[:, :, None], jnp.zeros((), route_weight.dtype)), axis=1)
    slot_index = jnp.cumsum(member, axis=0) - member
    slot_ids = jnp.arange(capacity, dtype=jnp.int32)
    picked = (slot_index.T[:, None, :] == slot_ids[None, :, None]) & (member.T[:, None, :] == 1)
    return picked.astype(jnp.float32), combine


def expert_stack(rows, gate_slices, up_slices, down_slices):
    total = jnp.zeros((rows.shape[0], down_slices.shape[2]), jnp.float32)
    for piece in range(SLICES):
        gate_val = jnp.dot(rows, gate_slices[piece], preferred_element_type=jnp.float32)
        up_val = jnp.dot(rows, up_slices[piece], preferred_element_type=jnp.float32)
        act = (jax.nn.silu(gate_val) * up_val).astype(jnp.bfloat16)
        partial_value = jnp.dot(act, down_slices[piece], preferred_element_type=jnp.float32).astype(jnp.bfloat16)
        total = total + partial_value.astype(jnp.float32)
    return total


def reference(tokens, routes, route_weight, w_gate, w_up, w_down, queries, latent_cache, lengths):
    blocks = N_NODE * N_DEV
    token_blocks = tokens.reshape(blocks, TOK, D)
    selector, combine = jax.vmap(lambda r, w: slot_tables(r, w, EXPERTS, CAP))(
        routes.reshape(blocks, TOK, TOP), route_weight.reshape(blocks, TOK, TOP))
    buffers = jnp.einsum('bect,btd->becd', selector, token_blocks.astype(jnp.float32)).astype(jnp.bfloat16)
    per_expert = buffers.transpose(1, 0, 2, 3).reshape(EXPERTS, blocks * CAP, D)
    gate_all = w_gate.reshape(EXPERTS, SLICES, D, HID_DEV)
    up_all = w_up.reshape(EXPERTS, SLICES, D, HID_DEV)
    down_all = w_down.reshape(EXPERTS, SLICES, HID_DEV, D)
    outputs = lax.map(lambda a: expert_stack(a[0], a[1], a[2], a[3]), (per_expert, gate_all, up_all, down_all))
    expert_out = outputs.reshape(EXPERTS, blocks, CAP, D).transpose(1, 0, 2, 3)
    weighted = selector * combine.transpose(0, 2, 1)[:, :, None, :]
    moe_out = jnp.einsum('bect,becd->btd', weighted, expert_out, precision=lax.Precision.HIGHEST)
    moe_out = moe_out.reshape(TOKENS, D).astype(jnp.bfloat16)
    score_scale = HEAD_QK ** -0.5
    scores = jnp.einsum('rhk,rlk->rhl', queries.astype(jnp.float32), latent_cache.astype(jnp.float32)) * score_scale
    visible = jnp.arange(LEN, dtype=jnp.int32)[None, None, :] < lengths[:, None, None]
    scores = jnp.where(visible, scores, -1e30)
    row_max = jnp.max(scores, axis=-1, keepdims=True)
    expo = jnp.exp(scores - row_max)
    row_sum = jnp.sum(expo, axis=-1, keepdims=True)
    weights_bf = (expo / row_sum).astype(jnp.bfloat16)
    context = jnp.einsum('rhl,rlk->rhk', weights_bf.astype(jnp.float32), latent_cache[:, :, :LAT].astype(jnp.float32))
    return moe_out, context.astype(jnp.bfloat16)
```

```python
import functools

import jax
import jax.numpy as jnp
from jax import lax
from jax.experimental import pallas as pl
from jax.experimental.pallas import tpu as pltpu
from jax.sharding import PartitionSpec as P

LAT = 512
HEAD_QK = 192
SLICES = 4
LANES = 128
PAIR = 2


def chunk_of(size, most):
    best = LANES
    for c in range(LANES, most + 1, LANES):
        if size % c == 0:
            best = c
    return best


def pack_kernel(experts_all, routes_ref, weight_ref, tokens_ref, out_ref):
    rows, width = tokens_ref.shape
    out_ref[:, :width] = tokens_ref[...]
    extra = out_ref.shape[1] - width
    column = lax.broadcasted_iota(jnp.int32, (rows, extra), 1)
    part = column // experts_all
    expert = (column - part * experts_all).astype(jnp.float32)
    square = (rows, rows)
    same = lax.broadcasted_iota(jnp.int32, square, 0) == lax.broadcasted_iota(jnp.int32, square, 1)

    def upright(row):
        return jnp.sum(jnp.where(same, row, 0.0), axis=1, keepdims=True)

    value = jnp.zeros((rows, extra), jnp.float32)
    for choice in range(routes_ref.shape[0]):
        named = upright(routes_ref[choice : choice + 1, :].astype(jnp.float32))
        value = value + jnp.where(named == expert, upright(weight_ref[choice : choice + 1, :]), 0.0)
    high = value.astype(jnp.bfloat16)
    rest = value - high.astype(jnp.float32)
    middle = rest.astype(jnp.bfloat16)
    low = (rest - middle.astype(jnp.float32)).astype(jnp.bfloat16)
    picked = jnp.where(
        part == 0,
        high.astype(jnp.float32),
        jnp.where(
            part == 1,
            middle.astype(jnp.float32),
            jnp.where(part == 2, low.astype(jnp.float32), 0.0),
        ),
    )
    out_ref[:, width:] = picked.astype(jnp.bfloat16)


def pack(tokens, routes, route_weight, experts_all):
    rows, width = tokens.shape
    extra = -(-3 * experts_all // LANES) * LANES
    return pl.pallas_call(
        functools.partial(pack_kernel, experts_all),
        out_shape=pltpu.VMEM((rows, width + extra), tokens.dtype),
        in_specs=[pl.BlockSpec(memory_space=pltpu.VMEM)] * 3,
        out_specs=pl.BlockSpec(memory_space=pltpu.VMEM),
        name="pack",
    )(routes.T, route_weight.T, tokens)


def expert_kernel(count, steps, *refs):
    blocks, masks = refs[:count], refs[count]
    weights = refs[count + 1 : count + 7]
    outs = refs[count + 7 : 2 * count + 7]
    rows, width = outs[0].shape
    depth = width // steps

    def columns(part):
        return jnp.concatenate([b[:, part] for b in blocks], axis=0)

    table = columns(pl.ds(width, blocks[0].shape[1] - width)).astype(jnp.float32)
    acts, scales = [], []
    for p in range(2):
        gate = up = None
        for k in range(steps):
            part = pl.ds(k * depth, depth)
            x = columns(part)
            g = jnp.dot(x, weights[3 * p][0, part, :], preferred_element_type=jnp.float32)
            u = jnp.dot(x, weights[3 * p + 1][0, part, :], preferred_element_type=jnp.float32)
            gate, up = (g, u) if gate is None else (gate + g, up + u)
        acts.append((jax.nn.silu(gate) * up).astype(jnp.bfloat16))
        scales.append(jnp.sum(table * masks[p : p + 1, :], axis=1, keepdims=True))
    for n in range(steps):
        part = pl.ds(n * depth, depth)
        total = None
        for p in range(2):
            value = scales[p] * jnp.dot(
                acts[p], weights[3 * p + 2][0, :, part], preferred_element_type=jnp.float32
            )
            total = value if total is None else total + value
        total = total.astype(jnp.bfloat16)
        for i, o in enumerate(outs):
            o[:, part] = total[i * rows : (i + 1) * rows]


def run_experts(blocks, masks, weights):
    count = len(blocks)
    rows, packed = blocks[0].shape
    width, hidden = weights[0].shape[1:]
    steps = width // chunk_of(width, 1024)
    return pl.pallas_call(
        functools.partial(expert_kernel, count, steps),
        out_shape=[pltpu.VMEM((rows, width), jnp.bfloat16)] * count,
        in_specs=[pl.BlockSpec(memory_space=pltpu.VMEM)] * (count + 7),
        out_specs=[pl.BlockSpec(memory_space=pltpu.VMEM)] * count,
        compiler_params=pltpu.CompilerParams(vmem_limit_bytes=2 * count * rows * packed + (16 << 20)),
        cost_estimate=pl.CostEstimate(
            flops=2 * count * rows * width * hidden * 6,
            bytes_accessed=2 * 6 * width * hidden,
            transcendentals=0,
        ),
        name="experts",
    )(
        *(pltpu.with_memory_space_constraint(b, pltpu.VMEM) for b in blocks),
        masks,
        *(pltpu.with_memory_space_constraint(w, pltpu.VMEM) for w in weights),
    )


def attend(queries, latent_cache, lengths):
    score_scale = HEAD_QK ** (-0.5)
    scores = (
        jnp.einsum("rhk,rlk->rhl", queries, latent_cache, preferred_element_type=jnp.float32)
        * score_scale
    )
    positions = jnp.arange(latent_cache.shape[1], dtype=jnp.int32)
    visible = positions[None, None, :] < lengths[:, None, None]
    scores = jnp.where(visible, scores, -1e30)
    row_max = jnp.max(scores, axis=-1, keepdims=True)
    expo = jnp.exp(scores - row_max)
    row_sum = jnp.sum(expo, axis=-1, keepdims=True)
    weights_bf = (expo / row_sum).astype(jnp.bfloat16)
    context = jnp.einsum(
        "rhl,rlk->rhk", weights_bf, latent_cache[:, :, :LAT], preferred_element_type=jnp.float32
    )
    return context.astype(jnp.bfloat16)


def add_all(*terms):
    total = terms[0].astype(jnp.float32)
    for t in terms[1:]:
        total = total + t.astype(jnp.float32)
    return total.astype(jnp.bfloat16)


def body(tokens, routes, route_weight, w_gate, w_up, w_down, queries, latent_cache, lengths):
    nodes, devs = lax.axis_size("node"), lax.axis_size("dev")
    experts_all = nodes * devs // SLICES
    lines = devs // PAIR

    def hop(value, offset):
        return lax.ppermute(value, "dev", [(d, d ^ offset) for d in range(devs)])

    def swap(value):
        return lax.ppermute(value, "node", [(i, i ^ 1) for i in range(nodes)])

    own = (w_gate, w_up, w_down)
    weights = own + tuple(swap(w) for w in own)
    dev, node = lax.axis_index("dev"), lax.axis_index("node")
    here = (node * devs + dev) // SLICES
    there = ((node ^ 1) * devs + dev) // SLICES

    packed = pack(tokens, routes, route_weight, experts_all)
    extra = packed.shape[1] - tokens.shape[1]
    column = jnp.arange(extra, dtype=jnp.int32)
    named = jnp.where(column < 3 * experts_all, column % experts_all, -1)
    masks = (named[None, :] == jnp.stack([here, there])[:, None]).astype(jnp.float32)

    gathered = {0: packed}
    bit = lines // 2
    while bit:
        for m in list(gathered):
            gathered[m ^ bit] = hop(gathered[m], bit * PAIR)
        bit //= 2
    keys = [(m, s) for m in range(lines) for s in range(PAIR)]
    blocks = [gathered[m] if s == 0 else hop(gathered[m], 1) for m, s in keys]

    partial = dict(zip(keys, run_experts(blocks, masks, weights), strict=True))
    context = attend(queries, latent_cache, lengths)

    terms = {m: [partial[m, 0]] for m in range(lines)}
    for m in reversed(range(lines)):
        terms[m].append(hop(partial[m, 1], 1))
    bit = 1
    while bit < lines:
        for m in sorted(terms, reverse=True):
            if m & bit:
                terms[m ^ bit].append(hop(add_all(*terms.pop(m)), bit * PAIR))
        bit *= 2
    return add_all(*terms[0]), context


def solution(mesh):
    return jax.shard_map(
        body,
        mesh=mesh,
        in_specs=(
            P(("parts", "node", "dev"), None),
            P(("parts", "node", "dev"), None),
            P(("parts", "node", "dev"), None),
            P(("node", "dev"), None, None),
            P(("node", "dev"), None, None),
            P(("node", "dev"), None, None),
            P(("parts", "node", "dev"), None, None),
            P(("parts", "node", "dev"), None, None),
            P(("parts", "node", "dev")),
        ),
        out_specs=(P(("parts", "node", "dev"), None), P(("parts", "node", "dev"), None, None)),
        check_vma=False,
    )
```

```python
import functools

import jax
import jax.numpy as jnp
from jax import lax
from jax.experimental import pallas as pl
from jax.experimental.pallas import tpu as pltpu
from jax.sharding import PartitionSpec as P

LAT = 512
HEAD_QK = 192
SLICES = 4
LANES = 128
CALL_ROWS = 256
PAIR = 2


def chunk_of(size, most):
    best = LANES
    for c in range(LANES, most + 1, LANES):
        if size % c == 0:
            best = c
    return best


def pack_kernel(experts_all, routes_hbm, weight_hbm, tokens_hbm, out_ref, routes_ref, weight_ref, sems):
    rows, width = tokens_hbm.shape
    copies = [
        pltpu.make_async_copy(tokens_hbm, out_ref.at[:, pl.ds(0, width)], sems.at[0]),
        pltpu.make_async_copy(routes_hbm, routes_ref, sems.at[1]),
        pltpu.make_async_copy(weight_hbm, weight_ref, sems.at[2]),
    ]
    for c in copies:
        c.start()
    copies[1].wait()
    copies[2].wait()
    extra = out_ref.shape[1] - width
    column = lax.broadcasted_iota(jnp.int32, (rows, extra), 1)
    part = column // experts_all
    expert = (column - part * experts_all).astype(jnp.float32)
    square = (rows, rows)
    same = lax.broadcasted_iota(jnp.int32, square, 0) == lax.broadcasted_iota(jnp.int32, square, 1)

    def upright(row):
        return jnp.sum(jnp.where(same, row, 0.0), axis=1, keepdims=True)

    value = jnp.zeros((rows, extra), jnp.float32)
    for choice in range(routes_ref.shape[0]):
        named = upright(routes_ref[choice : choice + 1, :].astype(jnp.float32))
        value = value + jnp.where(named == expert, upright(weight_ref[choice : choice + 1, :]), 0.0)
    high = value.astype(jnp.bfloat16)
    rest = value - high.astype(jnp.float32)
    middle = rest.astype(jnp.bfloat16)
    low = (rest - middle.astype(jnp.float32)).astype(jnp.bfloat16)
    picked = jnp.where(
        part == 0,
        high.astype(jnp.float32),
        jnp.where(
            part == 1,
            middle.astype(jnp.float32),
            jnp.where(part == 2, low.astype(jnp.float32), 0.0),
        ),
    )
    out_ref[:, width:] = picked.astype(jnp.bfloat16)
    copies[0].wait()


def pack(tokens, routes, route_weight, experts_all):
    rows, width = tokens.shape
    extra = -(-3 * experts_all // LANES) * LANES
    operands = (routes.T, route_weight.T, tokens)
    return pl.pallas_call(
        functools.partial(pack_kernel, experts_all),
        out_shape=pltpu.VMEM((rows, width + extra), tokens.dtype),
        in_specs=[pl.BlockSpec(memory_space=pltpu.HBM)] * 3,
        out_specs=pl.BlockSpec(memory_space=pltpu.VMEM),
        scratch_shapes=[
            pltpu.VMEM(routes.T.shape, routes.dtype),
            pltpu.VMEM(route_weight.T.shape, route_weight.dtype),
            pltpu.SemaphoreType.DMA((3,)),
        ],
        compiler_params=pltpu.CompilerParams(vmem_limit_bytes=2 << 20),
        name="pack",
    )(*(pltpu.with_memory_space_constraint(a, pltpu.HBM) for a in operands))


def expert_kernel(count, steps, *refs):
    blocks, mask = refs[:count], refs[count]
    gate_w, up_w, down_w = refs[count + 1 : count + 4]
    outs = refs[count + 4 :]
    width = outs[0].shape[1]
    rows = outs[0].shape[0]
    depth = width // steps

    def columns(part):
        return jnp.concatenate([b[:, part] for b in blocks], axis=0)

    table = columns(pl.ds(width, blocks[0].shape[1] - width)).astype(jnp.float32)
    scale = jnp.sum(table * mask[...], axis=1, keepdims=True)
    gate = up = None
    for k in range(steps):
        part = pl.ds(k * depth, depth)
        x = columns(part)
        g = jnp.dot(x, gate_w[0, part, :], preferred_element_type=jnp.float32)
        u = jnp.dot(x, up_w[0, part, :], preferred_element_type=jnp.float32)
        gate, up = (g, u) if gate is None else (gate + g, up + u)
    act = (jax.nn.silu(gate) * up).astype(jnp.bfloat16)
    for n in range(steps):
        part = pl.ds(n * depth, depth)
        value = scale * jnp.dot(act, down_w[0, :, part], preferred_element_type=jnp.float32)
        value = value.astype(jnp.bfloat16)
        for i, o in enumerate(outs):
            o[:, part] = value[i * rows : (i + 1) * rows]


def stage_kernel(count, *refs):
    sources, targets, sems = refs[:count], refs[count : 2 * count], refs[2 * count]
    copies = [
        pltpu.make_async_copy(a, b, sems.at[i])
        for i, (a, b) in enumerate(zip(sources, targets, strict=True))
    ]
    for c in copies:
        c.start()
    for c in copies:
        c.wait()


def stage(*arrays):
    count = len(arrays)
    return pl.pallas_call(
        functools.partial(stage_kernel, count),
        out_shape=[pltpu.VMEM(a.shape, a.dtype) for a in arrays],
        in_specs=[pl.BlockSpec(memory_space=pltpu.HBM)] * count,
        out_specs=[pl.BlockSpec(memory_space=pltpu.VMEM)] * count,
        scratch_shapes=[pltpu.SemaphoreType.DMA((count,))],
        compiler_params=pltpu.CompilerParams(vmem_limit_bytes=1 << 20),
        cost_estimate=pl.CostEstimate(
            flops=0, bytes_accessed=sum(2 * a.size for a in arrays), transcendentals=0
        ),
        name="stage",
    )(*(pltpu.with_memory_space_constraint(a, pltpu.HBM) for a in arrays))


def run_experts(blocks, group, mask, weights):
    count = len(blocks)
    rows, packed = blocks[0].shape
    width, hidden = weights[0].shape[1:]
    steps = width // chunk_of(width, 1024)
    pinned = [pltpu.with_memory_space_constraint(a, pltpu.VMEM) for a in (*blocks, mask, *weights)]
    return pl.pallas_call(
        functools.partial(expert_kernel, count, steps),
        out_shape=[pltpu.VMEM((group * rows, width), jnp.bfloat16)] * (count // group),
        in_specs=[pl.BlockSpec(memory_space=pltpu.VMEM)] * len(pinned),
        out_specs=[pl.BlockSpec(memory_space=pltpu.VMEM)] * (count // group),
        compiler_params=pltpu.CompilerParams(vmem_limit_bytes=2 * count * rows * packed + (16 << 20)),
        cost_estimate=pl.CostEstimate(
            flops=2 * count * rows * width * hidden * 3,
            bytes_accessed=2 * 3 * width * hidden,
            transcendentals=0,
        ),
        name="experts",
    )(*pinned)


def attend(queries, latent_cache, lengths):
    score_scale = HEAD_QK ** (-0.5)
    scores = (
        jnp.einsum("rhk,rlk->rhl", queries, latent_cache, preferred_element_type=jnp.float32)
        * score_scale
    )
    positions = jnp.arange(latent_cache.shape[1], dtype=jnp.int32)
    visible = positions[None, None, :] < lengths[:, None, None]
    scores = jnp.where(visible, scores, -1e30)
    row_max = jnp.max(scores, axis=-1, keepdims=True)
    expo = jnp.exp(scores - row_max)
    row_sum = jnp.sum(expo, axis=-1, keepdims=True)
    weights_bf = (expo / row_sum).astype(jnp.bfloat16)
    context = jnp.einsum(
        "rhl,rlk->rhk", weights_bf, latent_cache[:, :, :LAT], preferred_element_type=jnp.float32
    )
    return context.astype(jnp.bfloat16)


def add_all(*terms):
    total = terms[0].astype(jnp.float32)
    for t in terms[1:]:
        total = total + t.astype(jnp.float32)
    return total.astype(jnp.bfloat16)


def body(tokens, routes, route_weight, w_gate, w_up, w_down, queries, latent_cache, lengths):
    nodes, devs = lax.axis_size("node"), lax.axis_size("dev")
    experts_all = nodes * devs // SLICES
    lines = devs // PAIR

    def hop(value, offset):
        return lax.ppermute(value, "dev", [(d, d ^ offset) for d in range(devs)])

    def swap(value):
        return lax.ppermute(value, "node", [(i, i ^ 1) for i in range(nodes)])

    here = (lax.axis_index("node") * devs + lax.axis_index("dev")) // SLICES

    extra = -(-3 * experts_all // LANES) * LANES
    column = jnp.arange(extra, dtype=jnp.int32)
    named = jnp.where(column < 3 * experts_all, column % experts_all, -1)
    mask = (named == here).astype(jnp.float32)[None, :]
    barrier = lax.optimization_barrier
    tokens, mask = barrier((tokens, mask))
    packed = pack(tokens, routes, route_weight, experts_all)
    weights = stage(w_gate, w_up, w_down)

    barrier = lax.optimization_barrier
    gathered, across = {0: packed}, {}
    bit = lines // 2
    while bit:
        for m in list(gathered):
            gathered[m ^ bit] = hop(gathered[m], bit * PAIR)
        if bit == lines // 2:
            gathered[bit], weights = barrier((gathered[bit], weights))
        bit //= 2
    for m in range(lines):
        if m == 2:
            gathered[m], across[m - 1] = barrier((gathered[m], across[m - 1]))
        across[m] = hop(gathered[m], 1)
    keys = [(m, s) for m in range(lines) for s in range(PAIR)]
    mine = [(gathered, across)[s][m] for m, s in keys]
    theirs = [swap(x) for x in mine]

    rows = tokens.shape[0]
    batch = max(1, CALL_ROWS // (2 * PAIR * rows))
    kept, sent = [], []
    for first in range(0, lines, batch):
        cut = slice(PAIR * first, PAIR * (first + batch))
        sums = run_experts(mine[cut] + theirs[cut], PAIR, mask, weights)
        kept += sums[: len(sums) // 2]
        sent += sums[len(sums) // 2 :]
    context = attend(queries, latent_cache, lengths)

    terms, crossed = {}, {}
    for m in reversed(range(lines)):
        met = swap(sent[m])
        out = add_all(kept[m][rows:], met[rows:])
        if m + 2 in crossed:
            out, crossed[m + 2] = barrier((out, crossed[m + 2]))
        crossed[m] = hop(out, 1)
        terms[m] = [kept[m][:rows], met[:rows]]
    for m in range(lines):
        terms[m].append(crossed[m])
    bit = 1
    while bit < lines:
        for m in sorted(terms, reverse=True):
            if m & bit:
                terms[m ^ bit].append(hop(add_all(*terms.pop(m)), bit * PAIR))
        bit *= 2
    return add_all(*terms[0]), context


def solution(mesh):
    return jax.shard_map(
        body,
        mesh=mesh,
        in_specs=(
            P(("parts", "node", "dev"), None),
            P(("parts", "node", "dev"), None),
            P(("parts", "node", "dev"), None),
            P(("node", "dev"), None, None),
            P(("node", "dev"), None, None),
            P(("node", "dev"), None, None),
            P(("parts", "node", "dev"), None, None),
            P(("parts", "node", "dev"), None, None),
            P(("parts", "node", "dev")),
        ),
        out_specs=(P(("parts", "node", "dev"), None), P(("parts", "node", "dev"), None, None)),
        check_vma=False,
    )
```

```python
import functools

import jax
import jax.numpy as jnp
from jax import lax
from jax.experimental import pallas as pl
from jax.experimental.pallas import tpu as pltpu
from jax.sharding import PartitionSpec as P

LAT = 512
HEAD_QK = 192
SLICES = 4
LANES = 128
CALL_ROWS = 128
PAIR = 2


def chunk_of(size, most):
    best = LANES
    for c in range(LANES, most + 1, LANES):
        if size % c == 0:
            best = c
    return best


def pack_kernel(experts_all, routes_hbm, weight_hbm, tokens_hbm, out_ref, routes_ref, weight_ref, sems):
    rows, width = tokens_hbm.shape
    copies = [
        pltpu.make_async_copy(tokens_hbm, out_ref.at[:, pl.ds(0, width)], sems.at[0]),
        pltpu.make_async_copy(routes_hbm, routes_ref, sems.at[1]),
        pltpu.make_async_copy(weight_hbm, weight_ref, sems.at[2]),
    ]
    for c in copies:
        c.start()
    copies[1].wait()
    copies[2].wait()
    extra = out_ref.shape[1] - width
    column = lax.broadcasted_iota(jnp.int32, (rows, extra), 1)
    part = column // experts_all
    expert = (column - part * experts_all).astype(jnp.float32)
    square = (rows, rows)
    same = lax.broadcasted_iota(jnp.int32, square, 0) == lax.broadcasted_iota(jnp.int32, square, 1)

    def upright(row):
        return jnp.sum(jnp.where(same, row, 0.0), axis=1, keepdims=True)

    value = jnp.zeros((rows, extra), jnp.float32)
    for choice in range(routes_ref.shape[0]):
        named = upright(routes_ref[choice : choice + 1, :].astype(jnp.float32))
        value = value + jnp.where(named == expert, upright(weight_ref[choice : choice + 1, :]), 0.0)
    high = value.astype(jnp.bfloat16)
    rest = value - high.astype(jnp.float32)
    middle = rest.astype(jnp.bfloat16)
    low = (rest - middle.astype(jnp.float32)).astype(jnp.bfloat16)
    picked = jnp.where(
        part == 0,
        high.astype(jnp.float32),
        jnp.where(
            part == 1,
            middle.astype(jnp.float32),
            jnp.where(part == 2, low.astype(jnp.float32), 0.0),
        ),
    )
    out_ref[:, width:] = picked.astype(jnp.bfloat16)
    copies[0].wait()


def pack(tokens, routes, route_weight, experts_all):
    rows, width = tokens.shape
    extra = -(-3 * experts_all // LANES) * LANES
    operands = (routes.T, route_weight.T, tokens)
    return pl.pallas_call(
        functools.partial(pack_kernel, experts_all),
        out_shape=pltpu.VMEM((rows, width + extra), tokens.dtype),
        in_specs=[pl.BlockSpec(memory_space=pltpu.HBM)] * 3,
        out_specs=pl.BlockSpec(memory_space=pltpu.VMEM),
        scratch_shapes=[
            pltpu.VMEM(routes.T.shape, routes.dtype),
            pltpu.VMEM(route_weight.T.shape, route_weight.dtype),
            pltpu.SemaphoreType.DMA((3,)),
        ],
        compiler_params=pltpu.CompilerParams(vmem_limit_bytes=2 << 20),
        name="pack",
    )(*(pltpu.with_memory_space_constraint(a, pltpu.HBM) for a in operands))


def expert_kernel(count, steps, *refs):
    blocks, masks = refs[:count], refs[count]
    weights = refs[count + 1 : count + 7]
    outs = refs[count + 7 :]
    rows, width = outs[0].shape
    depth = width // steps
    parts = [pl.ds(k * depth, depth) for k in range(steps)]

    def columns(part):
        return jnp.concatenate([b[:, part] for b in blocks], axis=0)

    table = columns(pl.ds(width, blocks[0].shape[1] - width)).astype(jnp.float32)
    sums = None
    for part in parts:
        x = columns(part)
        new = [
            jnp.dot(x, weights[i][0, part, :], preferred_element_type=jnp.float32)
            for i in (0, 1, 3, 4)
        ]
        sums = new if sums is None else [a + b for a, b in zip(sums, new, strict=True)]
    acts, scales = [], []
    for p in range(2):
        gate, up = sums[2 * p : 2 * p + 2]
        acts.append((jax.nn.silu(gate) * up).astype(jnp.bfloat16))
        scales.append(jnp.sum(table * masks[p : p + 1, :], axis=1, keepdims=True))
    for part in parts:
        total = None
        for p in range(2):
            value = scales[p] * jnp.dot(
                acts[p], weights[3 * p + 2][0, :, part], preferred_element_type=jnp.float32
            )
            total = value if total is None else total + value
        total = total.astype(jnp.bfloat16)
        for i, o in enumerate(outs):
            o[:, part] = total[i * rows : (i + 1) * rows]


def stage_kernel(count, *refs):
    sources, targets, sems = refs[:count], refs[count : 2 * count], refs[2 * count]
    copies = [
        pltpu.make_async_copy(a, b, sems.at[i])
        for i, (a, b) in enumerate(zip(sources, targets, strict=True))
    ]
    for c in copies:
        c.start()
    for c in copies:
        c.wait()


def stage(*arrays):
    count = len(arrays)
    return pl.pallas_call(
        functools.partial(stage_kernel, count),
        out_shape=[pltpu.VMEM(a.shape, a.dtype) for a in arrays],
        in_specs=[pl.BlockSpec(memory_space=pltpu.HBM)] * count,
        out_specs=[pl.BlockSpec(memory_space=pltpu.VMEM)] * count,
        scratch_shapes=[pltpu.SemaphoreType.DMA((count,))],
        compiler_params=pltpu.CompilerParams(vmem_limit_bytes=1 << 20),
        cost_estimate=pl.CostEstimate(
            flops=0, bytes_accessed=sum(2 * a.size for a in arrays), transcendentals=0
        ),
        name="stage",
    )(*(pltpu.with_memory_space_constraint(a, pltpu.HBM) for a in arrays))


def run_experts(blocks, masks, weights):
    count = len(blocks)
    rows, packed = blocks[0].shape
    width, hidden = weights[0].shape[1:]
    steps = width // chunk_of(width, 1024)
    operands = [pltpu.with_memory_space_constraint(a, pltpu.VMEM) for a in (*blocks, masks, *weights)]
    return pl.pallas_call(
        functools.partial(expert_kernel, count, steps),
        out_shape=[pltpu.VMEM((rows, width), jnp.bfloat16)] * count,
        in_specs=[pl.BlockSpec(memory_space=pltpu.VMEM)] * len(operands),
        out_specs=[pl.BlockSpec(memory_space=pltpu.VMEM)] * count,
        compiler_params=pltpu.CompilerParams(vmem_limit_bytes=2 * count * rows * packed + (16 << 20)),
        cost_estimate=pl.CostEstimate(
            flops=2 * count * rows * width * hidden * 6,
            bytes_accessed=2 * 6 * width * hidden,
            transcendentals=0,
        ),
        name="experts",
    )(*operands)


def attend(queries, latent_cache, lengths):
    score_scale = HEAD_QK ** (-0.5)
    scores = (
        jnp.einsum("rhk,rlk->rhl", queries, latent_cache, preferred_element_type=jnp.float32)
        * score_scale
    )
    positions = jnp.arange(latent_cache.shape[1], dtype=jnp.int32)
    visible = positions[None, None, :] < lengths[:, None, None]
    scores = jnp.where(visible, scores, -1e30)
    row_max = jnp.max(scores, axis=-1, keepdims=True)
    expo = jnp.exp(scores - row_max)
    row_sum = jnp.sum(expo, axis=-1, keepdims=True)
    weights_bf = (expo / row_sum).astype(jnp.bfloat16)
    context = jnp.einsum(
        "rhl,rlk->rhk", weights_bf, latent_cache[:, :, :LAT], preferred_element_type=jnp.float32
    )
    return context.astype(jnp.bfloat16)


def add_all(*terms):
    total = terms[0].astype(jnp.float32)
    for t in terms[1:]:
        total = total + t.astype(jnp.float32)
    return total.astype(jnp.bfloat16)


def body(tokens, routes, route_weight, w_gate, w_up, w_down, queries, latent_cache, lengths):
    nodes, devs = lax.axis_size("node"), lax.axis_size("dev")
    experts_all = nodes * devs // SLICES
    lines = devs // PAIR

    def hop(value, offset):
        return lax.ppermute(value, "dev", [(d, d ^ offset) for d in range(devs)])

    def swap(value):
        return lax.ppermute(value, "node", [(i, i ^ 1) for i in range(nodes)])

    barrier = lax.optimization_barrier
    dev, node = lax.axis_index("dev"), lax.axis_index("node")
    experts_here = jnp.stack([n * devs + dev for n in (node, node ^ 1)]) // SLICES
    extra = -(-3 * experts_all // LANES) * LANES
    column = jnp.arange(extra, dtype=jnp.int32)
    named = jnp.where(column < 3 * experts_all, column % experts_all, -1)
    masks = (named[None, :] == experts_here[:, None]).astype(jnp.float32)
    tokens, masks = barrier((tokens, masks))
    packed = pack(tokens, routes, route_weight, experts_all)

    w_gate, w_up, packed = barrier((w_gate, w_up, packed))
    gate_there, up_there = swap(w_gate), swap(w_up)
    bits = [1 << i for i in reversed(range(lines.bit_length() - 1))]
    gathered, across = {0: packed}, {}
    for bit in bits:
        gathered[bit] = hop(packed, bit * PAIR)
    across[0] = hop(packed, 1)
    weights_here = stage(w_gate, w_up, w_down)
    gathered, across, weights_here, gate_there, up_there = barrier(
        (gathered, across, weights_here, gate_there, up_there)
    )
    w_down, gate_there = barrier((w_down, gate_there))
    down_there = swap(w_down)
    into_there = stage(gate_there, up_there)
    for bit in bits[1:]:
        for m in sorted(gathered):
            if m & -m > bit:
                gathered[m ^ bit] = hop(gathered[m], bit * PAIR)
    other, far, into_there = barrier((across[0], gathered[lines - 1], into_there))
    gathered[lines - 1] = far
    across[1] = hop(other, PAIR)
    for m in range(2, lines):
        across[m] = hop(gathered[m], 1)
    weights = (*weights_here, *into_there, *stage(down_there))

    rows = tokens.shape[0]
    batch = max(1, CALL_ROWS // (PAIR * rows))
    terms = {}
    for first in range(0, lines, batch):
        cut = [(m, s) for m in range(first, min(lines, first + batch)) for s in range(PAIR)]
        blocks = [(gathered, across)[s][m] for m, s in cut]
        for key, value in zip(cut, run_experts(blocks, masks, weights), strict=True):
            terms[key] = [value]
    context = attend(queries, latent_cache, lengths)

    aside = hop(add_all(*terms.pop((1, 1))), PAIR)
    before = None
    for m in reversed(range(lines)):
        if m == 1:
            continue
        out = add_all(*terms.pop((m, 1)))
        if before is not None:
            out, terms[before, 0][-1] = barrier((out, terms[before, 0][-1]))
        terms[m, 0].append(hop(out, 1))
        before = m
        if m == lines - 1:
            terms[0, 1].append(aside)
        elif m == lines - 2:
            terms[m, 0][-1], terms[0, 1][-1] = barrier((terms[m, 0][-1], terms[0, 1][-1]))
    for bit in reversed(bits):
        before = None
        for m in sorted([m for m, _ in terms if m & bit], reverse=True):
            out = add_all(*terms.pop((m, 0)))
            if before is not None:
                out, terms[before, 0][-1] = barrier((out, terms[before, 0][-1]))
            terms[m ^ bit, 0].append(hop(out, bit * PAIR))
            before = m ^ bit
    return add_all(*terms[0, 0]), context


def solution(mesh):
    return jax.shard_map(
        body,
        mesh=mesh,
        in_specs=(
            P(("parts", "node", "dev"), None),
            P(("parts", "node", "dev"), None),
            P(("parts", "node", "dev"), None),
            P(("node", "dev"), None, None),
            P(("node", "dev"), None, None),
            P(("node", "dev"), None, None),
            P(("parts", "node", "dev"), None, None),
            P(("parts", "node", "dev"), None, None),
            P(("parts", "node", "dev")),
        ),
        out_specs=(P(("parts", "node", "dev"), None), P(("parts", "node", "dev"), None, None)),
        check_vma=False,
    )
```

```python
import functools

import jax
import jax.numpy as jnp
from jax import lax
from jax.experimental import pallas as pl
from jax.experimental.pallas import tpu as pltpu
from jax.sharding import PartitionSpec as P

LAT = 512
HEAD_QK = 192
SLICES = 4
LANES = 128
CALL_ROWS = 128
PAIR = 2


def chunk_of(size, most):
    best = LANES
    for c in range(LANES, most + 1, LANES):
        if size % c == 0:
            best = c
    return best


def pack_kernel(experts_all, routes_hbm, weight_hbm, tokens_hbm, out_ref, routes_ref, weight_ref, sems):
    rows, width = tokens_hbm.shape
    copies = [
        pltpu.make_async_copy(tokens_hbm, out_ref.at[:, pl.ds(0, width)], sems.at[0]),
        pltpu.make_async_copy(routes_hbm, routes_ref, sems.at[1]),
        pltpu.make_async_copy(weight_hbm, weight_ref, sems.at[2]),
    ]
    for c in copies:
        c.start()
    copies[1].wait()
    copies[2].wait()
    extra = out_ref.shape[1] - width
    column = lax.broadcasted_iota(jnp.int32, (rows, extra), 1)
    part = column // experts_all
    expert = (column - part * experts_all).astype(jnp.float32)
    square = (rows, rows)
    same = lax.broadcasted_iota(jnp.int32, square, 0) == lax.broadcasted_iota(jnp.int32, square, 1)

    def upright(row):
        return jnp.sum(jnp.where(same, row, 0.0), axis=1, keepdims=True)

    value = jnp.zeros((rows, extra), jnp.float32)
    for choice in range(routes_ref.shape[0]):
        named = upright(routes_ref[choice : choice + 1, :].astype(jnp.float32))
        value = value + jnp.where(named == expert, upright(weight_ref[choice : choice + 1, :]), 0.0)
    high = value.astype(jnp.bfloat16)
    rest = value - high.astype(jnp.float32)
    middle = rest.astype(jnp.bfloat16)
    low = (rest - middle.astype(jnp.float32)).astype(jnp.bfloat16)
    picked = jnp.where(
        part == 0,
        high.astype(jnp.float32),
        jnp.where(
            part == 1,
            middle.astype(jnp.float32),
            jnp.where(part == 2, low.astype(jnp.float32), 0.0),
        ),
    )
    out_ref[:, width:] = picked.astype(jnp.bfloat16)
    copies[0].wait()


def pack(tokens, routes, route_weight, experts_all):
    rows, width = tokens.shape
    extra = -(-3 * experts_all // LANES) * LANES
    operands = (routes.T, route_weight.T, tokens)
    return pl.pallas_call(
        functools.partial(pack_kernel, experts_all),
        out_shape=pltpu.VMEM((rows, width + extra), tokens.dtype),
        in_specs=[pl.BlockSpec(memory_space=pltpu.HBM)] * 3,
        out_specs=pl.BlockSpec(memory_space=pltpu.VMEM),
        scratch_shapes=[
            pltpu.VMEM(routes.T.shape, routes.dtype),
            pltpu.VMEM(route_weight.T.shape, route_weight.dtype),
            pltpu.SemaphoreType.DMA((3,)),
        ],
        compiler_params=pltpu.CompilerParams(vmem_limit_bytes=2 << 20),
        name="pack",
    )(*(pltpu.with_memory_space_constraint(a, pltpu.HBM) for a in operands))


def expert_kernel(count, steps, *refs):
    blocks, masks = refs[:count], refs[count]
    weights = refs[count + 1 : count + 7]
    outs = refs[count + 7 :]
    rows, width = outs[0].shape
    depth = width // steps
    parts = [pl.ds(k * depth, depth) for k in range(steps)]

    def columns(part):
        return jnp.concatenate([b[:, part] for b in blocks], axis=0)

    table = columns(pl.ds(width, blocks[0].shape[1] - width)).astype(jnp.float32)
    sums = None
    for part in parts:
        x = columns(part)
        new = [
            jnp.dot(x, weights[i][0, part, :], preferred_element_type=jnp.float32)
            for i in (0, 1, 3, 4)
        ]
        sums = new if sums is None else [a + b for a, b in zip(sums, new, strict=True)]
    acts, scales = [], []
    for p in range(2):
        gate, up = sums[2 * p : 2 * p + 2]
        acts.append((jax.nn.silu(gate) * up).astype(jnp.bfloat16))
        scales.append(jnp.sum(table * masks[p : p + 1, :], axis=1, keepdims=True))
    for part in parts:
        total = None
        for p in range(2):
            value = scales[p] * jnp.dot(
                acts[p], weights[3 * p + 2][0, :, part], preferred_element_type=jnp.float32
            )
            total = value if total is None else total + value
        total = total.astype(jnp.bfloat16)
        for i, o in enumerate(outs):
            o[:, part] = total[i * rows : (i + 1) * rows]


def stage_kernel(count, *refs):
    sources, targets, sems = refs[:count], refs[count : 2 * count], refs[2 * count]
    copies = [
        pltpu.make_async_copy(a, b, sems.at[i])
        for i, (a, b) in enumerate(zip(sources, targets, strict=True))
    ]
    for c in copies:
        c.start()
    for c in copies:
        c.wait()


def stage(*arrays):
    count = len(arrays)
    return pl.pallas_call(
        functools.partial(stage_kernel, count),
        out_shape=[pltpu.VMEM(a.shape, a.dtype) for a in arrays],
        in_specs=[pl.BlockSpec(memory_space=pltpu.HBM)] * count,
        out_specs=[pl.BlockSpec(memory_space=pltpu.VMEM)] * count,
        scratch_shapes=[pltpu.SemaphoreType.DMA((count,))],
        compiler_params=pltpu.CompilerParams(vmem_limit_bytes=1 << 20),
        cost_estimate=pl.CostEstimate(
            flops=0, bytes_accessed=sum(2 * a.size for a in arrays), transcendentals=0
        ),
        name="stage",
    )(*(pltpu.with_memory_space_constraint(a, pltpu.HBM) for a in arrays))


def run_experts(blocks, masks, weights):
    count = len(blocks)
    rows, packed = blocks[0].shape
    width, hidden = weights[0].shape[1:]
    steps = width // chunk_of(width, 1024)
    operands = [pltpu.with_memory_space_constraint(a, pltpu.VMEM) for a in (*blocks, masks, *weights)]
    return pl.pallas_call(
        functools.partial(expert_kernel, count, steps),
        out_shape=[pltpu.VMEM((rows, width), jnp.bfloat16)] * count,
        in_specs=[pl.BlockSpec(memory_space=pltpu.VMEM)] * len(operands),
        out_specs=[pl.BlockSpec(memory_space=pltpu.VMEM)] * count,
        compiler_params=pltpu.CompilerParams(vmem_limit_bytes=2 * count * rows * packed + (16 << 20)),
        cost_estimate=pl.CostEstimate(
            flops=2 * count * rows * width * hidden * 6,
            bytes_accessed=2 * 6 * width * hidden,
            transcendentals=0,
        ),
        name="experts",
    )(*operands)


def probabilities(queries, latent_cache, lengths):
    score_scale = HEAD_QK ** (-0.5)
    scores = (
        jnp.einsum("rhk,rlk->rhl", queries, latent_cache, preferred_element_type=jnp.float32)
        * score_scale
    )
    positions = jnp.arange(latent_cache.shape[1], dtype=jnp.int32)
    visible = positions[None, None, :] < lengths[:, None, None]
    scores = jnp.where(visible, scores, -1e30)
    row_max = jnp.max(scores, axis=-1, keepdims=True)
    expo = jnp.exp(scores - row_max)
    row_sum = jnp.sum(expo, axis=-1, keepdims=True)
    return (expo / row_sum).astype(jnp.bfloat16)


def attend(probs, latent_cache):
    context = jnp.einsum(
        "rhl,rlk->rhk", probs, latent_cache[:, :, :LAT], preferred_element_type=jnp.float32
    )
    return context.astype(jnp.bfloat16)


def add_all(*terms):
    total = terms[0].astype(jnp.float32)
    for t in terms[1:]:
        total = total + t.astype(jnp.float32)
    return total.astype(jnp.bfloat16)


def body(tokens, routes, route_weight, w_gate, w_up, w_down, queries, latent_cache, lengths):
    nodes, devs = lax.axis_size("node"), lax.axis_size("dev")
    experts_all = nodes * devs // SLICES
    lines = devs // PAIR

    def hop(value, offset):
        return lax.ppermute(value, "dev", [(d, d ^ offset) for d in range(devs)])

    def swap(value):
        return lax.ppermute(value, "node", [(i, i ^ 1) for i in range(nodes)])

    barrier = lax.optimization_barrier
    dev, node = lax.axis_index("dev"), lax.axis_index("node")
    experts_here = jnp.stack([n * devs + dev for n in (node, node ^ 1)]) // SLICES
    extra = -(-3 * experts_all // LANES) * LANES
    column = jnp.arange(extra, dtype=jnp.int32)
    named = jnp.where(column < 3 * experts_all, column % experts_all, -1)
    masks = (named[None, :] == experts_here[:, None]).astype(jnp.float32)
    tokens, masks = barrier((tokens, masks))
    packed = pack(tokens, routes, route_weight, experts_all)

    w_gate, w_up, packed = barrier((w_gate, w_up, packed))
    gate_there, up_there = swap(w_gate), swap(w_up)
    bits = [1 << i for i in reversed(range(lines.bit_length() - 1))]
    gathered, across = {0: packed}, {}
    for bit in bits:
        gathered[bit] = hop(packed, (2 * bit - 1) * PAIR)
    across[0] = hop(packed, 1)
    weights_here = stage(w_gate, w_up, w_down)
    gathered, across, weights_here, gate_there = barrier(
        (gathered, across, weights_here, gate_there)
    )
    w_down, gate_there = barrier((w_down, gate_there))
    down_there = swap(w_down)
    into_there = stage(gate_there, up_there)
    for bit in bits[1:]:
        for m in sorted(gathered):
            if m & -m > bit:
                gathered[m ^ bit] = hop(gathered[m], (2 * bit - 1) * PAIR)
    other, far, into_there = barrier((across[0], gathered[lines - 1], into_there))
    gathered[lines - 1] = far
    across[1] = hop(other, PAIR)
    for m in range(2, lines):
        across[m] = hop(gathered[m], 1)
    weights = (*weights_here, *into_there, *stage(down_there))

    rows = tokens.shape[0]
    batch = max(1, CALL_ROWS // (PAIR * rows))
    terms = {}
    for first in range(0, lines, batch):
        cut = [(m, s) for m in range(first, min(lines, first + batch)) for s in range(PAIR)]
        blocks = [(gathered, across)[s][m] for m, s in cut]
        for key, value in zip(cut, run_experts(blocks, masks, weights), strict=True):
            terms[key] = [value]
    probs = probabilities(queries, latent_cache, lengths)

    aside = hop(add_all(*terms.pop((1, 1))), PAIR)
    before = None
    for m in reversed(range(lines)):
        if m == 1:
            continue
        out = add_all(*terms.pop((m, 1)))
        if before is not None:
            out, terms[before, 0][-1] = barrier((out, terms[before, 0][-1]))
        terms[m, 0].append(hop(out, 1))
        before = m
        if m == lines - 1:
            terms[0, 1].append(aside)
        elif m == lines - 2:
            terms[m, 0][-1], terms[0, 1][-1] = barrier((terms[m, 0][-1], terms[0, 1][-1]))
    for bit in reversed(bits):
        before = None
        for m in sorted([m for m, _ in terms if m & bit], reverse=True):
            out = add_all(*terms.pop((m, 0)))
            if before is not None:
                out, terms[before, 0][-1] = barrier((out, terms[before, 0][-1]))
            terms[m ^ bit, 0].append(hop(out, (2 * bit - 1) * PAIR))
            before = m ^ bit
        if bit == 1:
            probs, terms[0, 0][-1] = barrier((probs, terms[0, 0][-1]))
    return add_all(*terms[0, 0]), attend(probs, latent_cache)


def solution(mesh):
    return jax.shard_map(
        body,
        mesh=mesh,
        in_specs=(
            P(("parts", "node", "dev"), None),
            P(("parts", "node", "dev"), None),
            P(("parts", "node", "dev"), None),
            P(("node", "dev"), None, None),
            P(("node", "dev"), None, None),
            P(("node", "dev"), None, None),
            P(("parts", "node", "dev"), None, None),
            P(("parts", "node", "dev"), None, None),
            P(("parts", "node", "dev")),
        ),
        out_specs=(P(("parts", "node", "dev"), None), P(("parts", "node", "dev"), None, None)),
        check_vma=False,
    )
```

```python
import functools

import jax
import jax.numpy as jnp
from jax import lax
from jax.experimental import pallas as pl
from jax.experimental.pallas import tpu as pltpu
from jax.sharding import PartitionSpec as P

LAT = 512
HEAD_QK = 192
SLICES = 4
LANES = 128
CALL_ROWS = 128
PAIR = 2


def chunk_of(size, most):
    best = LANES
    for c in range(LANES, most + 1, LANES):
        if size % c == 0:
            best = c
    return best


def pack_kernel(experts_all, routes_hbm, weight_hbm, tokens_hbm, out_ref, routes_ref, weight_ref, sems):
    rows, width = tokens_hbm.shape
    copies = [
        pltpu.make_async_copy(tokens_hbm, out_ref.at[:, pl.ds(0, width)], sems.at[0]),
        pltpu.make_async_copy(routes_hbm, routes_ref, sems.at[1]),
        pltpu.make_async_copy(weight_hbm, weight_ref, sems.at[2]),
    ]
    for c in copies:
        c.start()
    copies[1].wait()
    copies[2].wait()
    extra = out_ref.shape[1] - width
    column = lax.broadcasted_iota(jnp.int32, (rows, extra), 1)
    part = column // experts_all
    expert = (column - part * experts_all).astype(jnp.float32)
    square = (rows, rows)
    same = lax.broadcasted_iota(jnp.int32, square, 0) == lax.broadcasted_iota(jnp.int32, square, 1)

    def upright(row):
        return jnp.sum(jnp.where(same, row, 0.0), axis=1, keepdims=True)

    value = jnp.zeros((rows, extra), jnp.float32)
    for choice in range(routes_ref.shape[0]):
        named = upright(routes_ref[choice : choice + 1, :].astype(jnp.float32))
        value = value + jnp.where(named == expert, upright(weight_ref[choice : choice + 1, :]), 0.0)
    high = value.astype(jnp.bfloat16)
    rest = value - high.astype(jnp.float32)
    middle = rest.astype(jnp.bfloat16)
    low = (rest - middle.astype(jnp.float32)).astype(jnp.bfloat16)
    picked = jnp.where(
        part == 0,
        high.astype(jnp.float32),
        jnp.where(
            part == 1,
            middle.astype(jnp.float32),
            jnp.where(part == 2, low.astype(jnp.float32), 0.0),
        ),
    )
    out_ref[:, width:] = picked.astype(jnp.bfloat16)
    copies[0].wait()


def pack(tokens, routes, route_weight, experts_all):
    rows, width = tokens.shape
    extra = -(-3 * experts_all // LANES) * LANES
    operands = (routes.T, route_weight.T, tokens)
    return pl.pallas_call(
        functools.partial(pack_kernel, experts_all),
        out_shape=pltpu.VMEM((rows, width + extra), tokens.dtype),
        in_specs=[pl.BlockSpec(memory_space=pltpu.HBM)] * 3,
        out_specs=pl.BlockSpec(memory_space=pltpu.VMEM),
        scratch_shapes=[
            pltpu.VMEM(routes.T.shape, routes.dtype),
            pltpu.VMEM(route_weight.T.shape, route_weight.dtype),
            pltpu.SemaphoreType.DMA((3,)),
        ],
        compiler_params=pltpu.CompilerParams(vmem_limit_bytes=2 << 20),
        name="pack",
    )(*(pltpu.with_memory_space_constraint(a, pltpu.HBM) for a in operands))


def expert_kernel(count, steps, *refs):
    blocks, masks = refs[:count], refs[count]
    weights = refs[count + 1 : count + 7]
    outs = refs[count + 7 :]
    rows, width = outs[0].shape
    depth = width // steps
    parts = [pl.ds(k * depth, depth) for k in range(steps)]

    def columns(part):
        return jnp.concatenate([b[:, part] for b in blocks], axis=0)

    table = columns(pl.ds(width, blocks[0].shape[1] - width)).astype(jnp.float32)
    sums = None
    for part in parts:
        x = columns(part)
        new = [
            jnp.dot(x, weights[i][0, part, :], preferred_element_type=jnp.float32)
            for i in (0, 1, 3, 4)
        ]
        sums = new if sums is None else [a + b for a, b in zip(sums, new, strict=True)]
    acts, scales = [], []
    for p in range(2):
        gate, up = sums[2 * p : 2 * p + 2]
        acts.append((jax.nn.silu(gate) * up).astype(jnp.bfloat16))
        scales.append(jnp.sum(table * masks[p : p + 1, :], axis=1, keepdims=True))
    for part in parts:
        total = None
        for p in range(2):
            value = scales[p] * jnp.dot(
                acts[p], weights[3 * p + 2][0, :, part], preferred_element_type=jnp.float32
            )
            total = value if total is None else total + value
        total = total.astype(jnp.bfloat16)
        for i, o in enumerate(outs):
            o[:, part] = total[i * rows : (i + 1) * rows]


def stage_kernel(count, *refs):
    sources, targets, sems = refs[:count], refs[count : 2 * count], refs[2 * count]
    copies = [
        pltpu.make_async_copy(a, b, sems.at[i])
        for i, (a, b) in enumerate(zip(sources, targets, strict=True))
    ]
    for c in copies:
        c.start()
    for c in copies:
        c.wait()


def stage(*arrays):
    count = len(arrays)
    return pl.pallas_call(
        functools.partial(stage_kernel, count),
        out_shape=[pltpu.VMEM(a.shape, a.dtype) for a in arrays],
        in_specs=[pl.BlockSpec(memory_space=pltpu.HBM)] * count,
        out_specs=[pl.BlockSpec(memory_space=pltpu.VMEM)] * count,
        scratch_shapes=[pltpu.SemaphoreType.DMA((count,))],
        compiler_params=pltpu.CompilerParams(vmem_limit_bytes=1 << 20),
        cost_estimate=pl.CostEstimate(
            flops=0, bytes_accessed=sum(2 * a.size for a in arrays), transcendentals=0
        ),
        name="stage",
    )(*(pltpu.with_memory_space_constraint(a, pltpu.HBM) for a in arrays))


def run_experts(blocks, masks, weights):
    count = len(blocks)
    rows, packed = blocks[0].shape
    width, hidden = weights[0].shape[1:]
    steps = width // chunk_of(width, 1792)
    operands = [pltpu.with_memory_space_constraint(a, pltpu.VMEM) for a in (*blocks, masks, *weights)]
    return pl.pallas_call(
        functools.partial(expert_kernel, count, steps),
        out_shape=[pltpu.VMEM((rows, width), jnp.bfloat16)] * count,
        in_specs=[pl.BlockSpec(memory_space=pltpu.VMEM)] * len(operands),
        out_specs=[pl.BlockSpec(memory_space=pltpu.VMEM)] * count,
        compiler_params=pltpu.CompilerParams(vmem_limit_bytes=2 * count * rows * packed + (16 << 20)),
        cost_estimate=pl.CostEstimate(
            flops=2 * count * rows * width * hidden * 6,
            bytes_accessed=2 * 6 * width * hidden,
            transcendentals=0,
        ),
        name="experts",
    )(*operands)


def probabilities(queries, latent_cache, lengths):
    score_scale = HEAD_QK ** (-0.5)
    scores = (
        jnp.einsum("rhk,rlk->rhl", queries, latent_cache, preferred_element_type=jnp.float32)
        * score_scale
    )
    positions = jnp.arange(latent_cache.shape[1], dtype=jnp.int32)
    visible = positions[None, None, :] < lengths[:, None, None]
    scores = jnp.where(visible, scores, -1e30)
    row_max = jnp.max(scores, axis=-1, keepdims=True)
    expo = jnp.exp(scores - row_max)
    row_sum = jnp.sum(expo, axis=-1, keepdims=True)
    return (expo / row_sum).astype(jnp.bfloat16)


def attend(probs, latent_cache):
    context = jnp.einsum(
        "rhl,rlk->rhk", probs, latent_cache[:, :, :LAT], preferred_element_type=jnp.float32
    )
    return context.astype(jnp.bfloat16)


def add_all(*terms):
    total = terms[0].astype(jnp.float32)
    for t in terms[1:]:
        total = total + t.astype(jnp.float32)
    return total.astype(jnp.bfloat16)


def body(tokens, routes, route_weight, w_gate, w_up, w_down, queries, latent_cache, lengths):
    nodes, devs = lax.axis_size("node"), lax.axis_size("dev")
    experts_all = nodes * devs // SLICES
    lines = devs // PAIR

    def hop(value, offset):
        return lax.ppermute(value, "dev", [(d, d ^ offset) for d in range(devs)])

    def swap(value):
        return lax.ppermute(value, "node", [(i, i ^ 1) for i in range(nodes)])

    barrier = lax.optimization_barrier
    dev, node = lax.axis_index("dev"), lax.axis_index("node")
    experts_here = jnp.stack([n * devs + dev for n in (node, node ^ 1)]) // SLICES
    extra = -(-3 * experts_all // LANES) * LANES
    column = jnp.arange(extra, dtype=jnp.int32)
    named = jnp.where(column < 3 * experts_all, column % experts_all, -1)
    masks = (named[None, :] == experts_here[:, None]).astype(jnp.float32)
    packed = pack(tokens, routes, route_weight, experts_all)

    w_gate, w_up, packed = barrier((w_gate, w_up, packed))
    w_down, masks = barrier((w_down, masks))
    gate_there, up_there = swap(w_gate), swap(w_up)
    bits = [1 << i for i in reversed(range(lines.bit_length() - 1))]
    gathered, across = {0: packed}, {}
    for bit in bits:
        gathered[bit] = hop(packed, (2 * bit - 1) * PAIR)
    across[0] = hop(packed, 1)
    weights_here = stage(w_gate, w_up, w_down)
    gathered, across, weights_here, gate_there = barrier(
        (gathered, across, weights_here, gate_there)
    )
    w_down, gate_there = barrier((w_down, gate_there))
    down_there = swap(w_down)
    into_there = stage(gate_there, up_there)
    for bit in bits[1:]:
        for m in sorted(gathered):
            if m & -m > bit:
                gathered[m ^ bit] = hop(gathered[m], (2 * bit - 1) * PAIR)
    other, far, into_there = barrier((across[0], gathered[lines - 1], into_there))
    gathered[lines - 1] = far
    across[1] = hop(other, PAIR)
    for m in range(2, lines):
        across[m] = hop(gathered[m], 1)
    weights = (*weights_here, *into_there, *stage(down_there))

    rows = tokens.shape[0]
    batch = max(1, CALL_ROWS // (PAIR * rows))
    terms = {}
    for first in range(0, lines, batch):
        cut = [(m, s) for m in range(first, min(lines, first + batch)) for s in range(PAIR)]
        blocks = [(gathered, across)[s][m] for m, s in cut]
        for key, value in zip(cut, run_experts(blocks, masks, weights), strict=True):
            terms[key] = [value]
    probs = probabilities(queries, latent_cache, lengths)

    aside = hop(add_all(*terms.pop((1, 1))), PAIR)
    before = None
    for m in reversed(range(lines)):
        if m == 1:
            continue
        out = add_all(*terms.pop((m, 1)))
        if before is not None:
            out, terms[before, 0][-1] = barrier((out, terms[before, 0][-1]))
        terms[m, 0].append(hop(out, 1))
        before = m
        if m == lines - 1:
            terms[0, 1].append(aside)
        elif m == lines - 2:
            terms[m, 0][-1], terms[0, 1][-1] = barrier((terms[m, 0][-1], terms[0, 1][-1]))
    for bit in reversed(bits):
        before = None
        for m in sorted([m for m, _ in terms if m & bit], reverse=True):
            out = add_all(*terms.pop((m, 0)))
            if before is not None:
                out, terms[before, 0][-1] = barrier((out, terms[before, 0][-1]))
            terms[m ^ bit, 0].append(hop(out, (2 * bit - 1) * PAIR))
            before = m ^ bit
        if bit == 1:
            probs, terms[0, 0][-1] = barrier((probs, terms[0, 0][-1]))
    return add_all(*terms[0, 0]), attend(probs, latent_cache)


def solution(mesh):
    return jax.shard_map(
        body,
        mesh=mesh,
        in_specs=(
            P(("parts", "node", "dev"), None),
            P(("parts", "node", "dev"), None),
            P(("parts", "node", "dev"), None),
            P(("node", "dev"), None, None),
            P(("node", "dev"), None, None),
            P(("node", "dev"), None, None),
            P(("parts", "node", "dev"), None, None),
            P(("parts", "node", "dev"), None, None),
            P(("parts", "node", "dev")),
        ),
        out_specs=(P(("parts", "node", "dev"), None), P(("parts", "node", "dev"), None, None)),
        check_vma=False,
    )
```

```python
import functools

import jax
import jax.numpy as jnp
from jax import lax
from jax.experimental import pallas as pl
from jax.experimental.pallas import tpu as pltpu
from jax.sharding import PartitionSpec as P

LAT = 512
HEAD_QK = 192
SLICES = 4
LANES = 128
CALL_ROWS = 128
PAIR = 2


def chunk_of(size, most):
    best = LANES
    for c in range(LANES, most + 1, LANES):
        if size % c == 0:
            best = c
    return best


def pack_kernel(experts_all, routes_hbm, weight_hbm, tokens_hbm, out_ref, routes_ref, weight_ref, sems):
    rows, width = tokens_hbm.shape
    copies = [
        pltpu.make_async_copy(tokens_hbm, out_ref.at[:, pl.ds(0, width)], sems.at[0]),
        pltpu.make_async_copy(routes_hbm, routes_ref, sems.at[1]),
        pltpu.make_async_copy(weight_hbm, weight_ref, sems.at[2]),
    ]
    for c in copies:
        c.start()
    copies[1].wait()
    copies[2].wait()
    extra = out_ref.shape[1] - width
    column = lax.broadcasted_iota(jnp.int32, (rows, extra), 1)
    part = column // experts_all
    expert = (column - part * experts_all).astype(jnp.float32)
    square = (rows, rows)
    same = lax.broadcasted_iota(jnp.int32, square, 0) == lax.broadcasted_iota(jnp.int32, square, 1)

    def upright(row):
        return jnp.sum(jnp.where(same, row, 0.0), axis=1, keepdims=True)

    value = jnp.zeros((rows, extra), jnp.float32)
    for choice in range(routes_ref.shape[0]):
        named = upright(routes_ref[choice : choice + 1, :].astype(jnp.float32))
        value = value + jnp.where(named == expert, upright(weight_ref[choice : choice + 1, :]), 0.0)
    high = value.astype(jnp.bfloat16)
    rest = value - high.astype(jnp.float32)
    middle = rest.astype(jnp.bfloat16)
    low = (rest - middle.astype(jnp.float32)).astype(jnp.bfloat16)
    picked = jnp.where(
        part == 0,
        high.astype(jnp.float32),
        jnp.where(
            part == 1,
            middle.astype(jnp.float32),
            jnp.where(part == 2, low.astype(jnp.float32), 0.0),
        ),
    )
    out_ref[:, width:] = picked.astype(jnp.bfloat16)
    copies[0].wait()


def pack(tokens, routes, route_weight, experts_all):
    rows, width = tokens.shape
    extra = -(-3 * experts_all // LANES) * LANES
    operands = (routes.T, route_weight.T, tokens)
    return pl.pallas_call(
        functools.partial(pack_kernel, experts_all),
        out_shape=pltpu.VMEM((rows, width + extra), tokens.dtype),
        in_specs=[pl.BlockSpec(memory_space=pltpu.HBM)] * 3,
        out_specs=pl.BlockSpec(memory_space=pltpu.VMEM),
        scratch_shapes=[
            pltpu.VMEM(routes.T.shape, routes.dtype),
            pltpu.VMEM(route_weight.T.shape, route_weight.dtype),
            pltpu.SemaphoreType.DMA((3,)),
        ],
        compiler_params=pltpu.CompilerParams(vmem_limit_bytes=2 << 20),
        name="pack",
    )(*(pltpu.with_memory_space_constraint(a, pltpu.HBM) for a in operands))


def expert_kernel(count, steps, *refs):
    blocks, masks = refs[:count], refs[count]
    weights = refs[count + 1 : count + 7]
    outs = refs[count + 7 :]
    rows, width = outs[0].shape
    depth = width // steps
    parts = [pl.ds(k * depth, depth) for k in range(steps)]

    def columns(part):
        return jnp.concatenate([b[:, part] for b in blocks], axis=0)

    table = columns(pl.ds(width, blocks[0].shape[1] - width)).astype(jnp.float32)
    sums = None
    for part in parts:
        x = columns(part)
        new = [
            jnp.dot(x, weights[i][0, part, :], preferred_element_type=jnp.float32)
            for i in (0, 1, 3, 4)
        ]
        sums = new if sums is None else [a + b for a, b in zip(sums, new, strict=True)]
    acts, scales = [], []
    for p in range(2):
        gate, up = sums[2 * p : 2 * p + 2]
        acts.append((jax.nn.silu(gate) * up).astype(jnp.bfloat16))
        scales.append(jnp.sum(table * masks[p : p + 1, :], axis=1, keepdims=True))
    for part in parts:
        total = None
        for p in range(2):
            value = scales[p] * jnp.dot(
                acts[p], weights[3 * p + 2][0, :, part], preferred_element_type=jnp.float32
            )
            total = value if total is None else total + value
        total = total.astype(jnp.bfloat16)
        for i, o in enumerate(outs):
            o[:, part] = total[i * rows : (i + 1) * rows]


def stage_kernel(count, *refs):
    sources, targets, sems = refs[:count], refs[count : 2 * count], refs[2 * count]
    copies = [
        pltpu.make_async_copy(a, b, sems.at[i])
        for i, (a, b) in enumerate(zip(sources, targets, strict=True))
    ]
    for c in copies:
        c.start()
    for c in copies:
        c.wait()


def stage(*arrays):
    count = len(arrays)
    return pl.pallas_call(
        functools.partial(stage_kernel, count),
        out_shape=[pltpu.VMEM(a.shape, a.dtype) for a in arrays],
        in_specs=[pl.BlockSpec(memory_space=pltpu.HBM)] * count,
        out_specs=[pl.BlockSpec(memory_space=pltpu.VMEM)] * count,
        scratch_shapes=[pltpu.SemaphoreType.DMA((count,))],
        compiler_params=pltpu.CompilerParams(vmem_limit_bytes=1 << 20),
        cost_estimate=pl.CostEstimate(
            flops=0, bytes_accessed=sum(2 * a.size for a in arrays), transcendentals=0
        ),
        name="stage",
    )(*(pltpu.with_memory_space_constraint(a, pltpu.HBM) for a in arrays))


def run_experts(blocks, masks, weights):
    count = len(blocks)
    rows, packed = blocks[0].shape
    width, hidden = weights[0].shape[1:]
    steps = width // chunk_of(width, 1024)
    operands = [pltpu.with_memory_space_constraint(a, pltpu.VMEM) for a in (*blocks, masks, *weights)]
    return pl.pallas_call(
        functools.partial(expert_kernel, count, steps),
        out_shape=[pltpu.VMEM((rows, width), jnp.bfloat16)] * count,
        in_specs=[pl.BlockSpec(memory_space=pltpu.VMEM)] * len(operands),
        out_specs=[pl.BlockSpec(memory_space=pltpu.VMEM)] * count,
        compiler_params=pltpu.CompilerParams(vmem_limit_bytes=2 * count * rows * packed + (16 << 20)),
        cost_estimate=pl.CostEstimate(
            flops=2 * count * rows * width * hidden * 6,
            bytes_accessed=2 * 6 * width * hidden,
            transcendentals=0,
        ),
        name="experts",
    )(*operands)


def probabilities(queries, latent_cache, lengths):
    score_scale = HEAD_QK ** (-0.5)
    scores = (
        jnp.einsum("rhk,rlk->rhl", queries, latent_cache, preferred_element_type=jnp.float32)
        * score_scale
    )
    positions = jnp.arange(latent_cache.shape[1], dtype=jnp.int32)
    visible = positions[None, None, :] < lengths[:, None, None]
    scores = jnp.where(visible, scores, -1e30)
    row_max = jnp.max(scores, axis=-1, keepdims=True)
    expo = jnp.exp(scores - row_max)
    row_sum = jnp.sum(expo, axis=-1, keepdims=True)
    return (expo / row_sum).astype(jnp.bfloat16)


def attend(probs, latent_cache):
    context = jnp.einsum(
        "rhl,rlk->rhk", probs, latent_cache[:, :, :LAT], preferred_element_type=jnp.float32
    )
    return context.astype(jnp.bfloat16)


def add_all(*terms):
    total = terms[0].astype(jnp.float32)
    for t in terms[1:]:
        total = total + t.astype(jnp.float32)
    return total.astype(jnp.bfloat16)


def body(tokens, routes, route_weight, w_gate, w_up, w_down, queries, latent_cache, lengths):
    nodes, devs = lax.axis_size("node"), lax.axis_size("dev")
    experts_all = nodes * devs // SLICES
    lines = devs // PAIR

    def hop(value, offset):
        return lax.ppermute(value, "dev", [(d, d ^ offset) for d in range(devs)])

    def swap(value):
        return lax.ppermute(value, "node", [(i, i ^ 1) for i in range(nodes)])

    barrier = lax.optimization_barrier
    dev, node = lax.axis_index("dev"), lax.axis_index("node")
    experts_here = jnp.stack([n * devs + dev for n in (node, node ^ 1)]) // SLICES
    extra = -(-3 * experts_all // LANES) * LANES
    column = jnp.arange(extra, dtype=jnp.int32)
    named = jnp.where(column < 3 * experts_all, column % experts_all, -1)
    masks = (named[None, :] == experts_here[:, None]).astype(jnp.float32)
    tokens, masks = barrier((tokens, masks))
    packed = pack(tokens, routes, route_weight, experts_all)

    w_gate, w_up, packed = barrier((w_gate, w_up, packed))
    gate_there, up_there = swap(w_gate), swap(w_up)
    bits = [1 << i for i in reversed(range(lines.bit_length() - 1))]
    gathered, across = {0: packed}, {}
    for bit in bits:
        gathered[bit] = hop(packed, (2 * bit - 1) * PAIR)
    across[0] = hop(packed, 1)
    weights_here = stage(w_gate, w_up, w_down)
    gathered, weights_here, gate_there = barrier((gathered, weights_here, gate_there))
    down_there = swap(w_down)
    into_there = stage(gate_there, up_there)
    for bit in bits[1:]:
        for m in sorted(gathered):
            if m & -m > bit:
                gathered[m ^ bit] = hop(gathered[m], (2 * bit - 1) * PAIR)
    other, far, into_there = barrier((across[0], gathered[lines - 1], into_there))
    gathered[lines - 1] = far
    across[1] = hop(other, PAIR)
    for m in range(2, lines):
        across[m] = hop(gathered[m], 1)
    weights = (*weights_here, *into_there, *stage(down_there))

    rows = tokens.shape[0]
    batch = max(1, CALL_ROWS // (PAIR * rows))
    terms = {}
    for first in range(0, lines, batch):
        cut = [(m, s) for m in range(first, min(lines, first + batch)) for s in range(PAIR)]
        blocks = [(gathered, across)[s][m] for m, s in cut]
        for key, value in zip(cut, run_experts(blocks, masks, weights), strict=True):
            terms[key] = [value]
    probs = probabilities(queries, latent_cache, lengths)

    aside = hop(add_all(*terms.pop((1, 1))), PAIR)
    before = None
    for m in reversed(range(lines)):
        if m == 1:
            continue
        out = add_all(*terms.pop((m, 1)))
        if before is not None:
            out, terms[before, 0][-1] = barrier((out, terms[before, 0][-1]))
        terms[m, 0].append(hop(out, 1))
        before = m
        if m == lines - 1:
            terms[0, 1].append(aside)
        elif m == lines - 2:
            terms[m, 0][-1], terms[0, 1][-1] = barrier((terms[m, 0][-1], terms[0, 1][-1]))
    for bit in reversed(bits):
        before = None
        for m in sorted([m for m, _ in terms if m & bit], reverse=True):
            out = add_all(*terms.pop((m, 0)))
            if before is not None:
                out, terms[before, 0][-1] = barrier((out, terms[before, 0][-1]))
            terms[m ^ bit, 0].append(hop(out, (2 * bit - 1) * PAIR))
            before = m ^ bit
        if bit == 1:
            probs, terms[0, 0][-1] = barrier((probs, terms[0, 0][-1]))
    return add_all(*terms[0, 0]), attend(probs, latent_cache)


def solution(mesh):
    return jax.shard_map(
        body,
        mesh=mesh,
        in_specs=(
            P(("parts", "node", "dev"), None),
            P(("parts", "node", "dev"), None),
            P(("parts", "node", "dev"), None),
            P(("node", "dev"), None, None),
            P(("node", "dev"), None, None),
            P(("node", "dev"), None, None),
            P(("parts", "node", "dev"), None, None),
            P(("parts", "node", "dev"), None, None),
            P(("parts", "node", "dev")),
        ),
        out_specs=(P(("parts", "node", "dev"), None), P(("parts", "node", "dev"), None, None)),
        check_vma=False,
    )
```

```python
import functools

import jax
import jax.numpy as jnp
from jax import lax
from jax.experimental import pallas as pl
from jax.experimental.pallas import tpu as pltpu
from jax.sharding import PartitionSpec as P

LAT = 512
HEAD_QK = 192
SLICES = 4
LANES = 128
CALL_ROWS = 128
PAIR = 2


def chunk_of(size, most):
    best = LANES
    for c in range(LANES, most + 1, LANES):
        if size % c == 0:
            best = c
    return best


def pack_kernel(experts_all, routes_hbm, weight_hbm, tokens_hbm, out_ref, routes_ref, weight_ref, sems):
    rows, width = tokens_hbm.shape
    copies = [
        pltpu.make_async_copy(tokens_hbm, out_ref.at[:, pl.ds(0, width)], sems.at[0]),
        pltpu.make_async_copy(routes_hbm, routes_ref, sems.at[1]),
        pltpu.make_async_copy(weight_hbm, weight_ref, sems.at[2]),
    ]
    for c in copies:
        c.start()
    copies[1].wait()
    copies[2].wait()
    extra = out_ref.shape[1] - width
    column = lax.broadcasted_iota(jnp.int32, (rows, extra), 1)
    part = column // experts_all
    expert = (column - part * experts_all).astype(jnp.float32)
    square = (rows, rows)
    same = lax.broadcasted_iota(jnp.int32, square, 0) == lax.broadcasted_iota(jnp.int32, square, 1)

    def upright(row):
        return jnp.sum(jnp.where(same, row, 0.0), axis=1, keepdims=True)

    value = jnp.zeros((rows, extra), jnp.float32)
    for choice in range(routes_ref.shape[0]):
        named = upright(routes_ref[choice : choice + 1, :].astype(jnp.float32))
        value = value + jnp.where(named == expert, upright(weight_ref[choice : choice + 1, :]), 0.0)
    high = value.astype(jnp.bfloat16)
    rest = value - high.astype(jnp.float32)
    middle = rest.astype(jnp.bfloat16)
    low = (rest - middle.astype(jnp.float32)).astype(jnp.bfloat16)
    picked = jnp.where(
        part == 0,
        high.astype(jnp.float32),
        jnp.where(
            part == 1,
            middle.astype(jnp.float32),
            jnp.where(part == 2, low.astype(jnp.float32), 0.0),
        ),
    )
    out_ref[:, width:] = picked.astype(jnp.bfloat16)
    copies[0].wait()


def pack(tokens, routes, route_weight, experts_all):
    rows, width = tokens.shape
    extra = -(-3 * experts_all // LANES) * LANES
    operands = (routes.T, route_weight.T, tokens)
    return pl.pallas_call(
        functools.partial(pack_kernel, experts_all),
        out_shape=pltpu.VMEM((rows, width + extra), tokens.dtype),
        in_specs=[pl.BlockSpec(memory_space=pltpu.HBM)] * 3,
        out_specs=pl.BlockSpec(memory_space=pltpu.VMEM),
        scratch_shapes=[
            pltpu.VMEM(routes.T.shape, routes.dtype),
            pltpu.VMEM(route_weight.T.shape, route_weight.dtype),
            pltpu.SemaphoreType.DMA((3,)),
        ],
        compiler_params=pltpu.CompilerParams(vmem_limit_bytes=2 << 20),
        name="pack",
    )(*(pltpu.with_memory_space_constraint(a, pltpu.HBM) for a in operands))


def expert_kernel(count, steps, *refs):
    blocks, masks = refs[:count], refs[count]
    weights = refs[count + 1 : count + 7]
    outs = refs[count + 7 :]
    rows, width = outs[0].shape
    depth = width // steps
    parts = [pl.ds(k * depth, depth) for k in range(steps)]

    def columns(part):
        return jnp.concatenate([b[:, part] for b in blocks], axis=0)

    table = columns(pl.ds(width, blocks[0].shape[1] - width)).astype(jnp.float32)
    sums = None
    for part in parts:
        x = columns(part)
        new = [
            jnp.dot(x, weights[i][0, part, :], preferred_element_type=jnp.float32)
            for i in (0, 1, 3, 4)
        ]
        sums = new if sums is None else [a + b for a, b in zip(sums, new, strict=True)]
    acts, scales = [], []
    for p in range(2):
        gate, up = sums[2 * p : 2 * p + 2]
        acts.append((jax.nn.silu(gate) * up).astype(jnp.bfloat16))
        scales.append(jnp.sum(table * masks[p : p + 1, :], axis=1, keepdims=True))
    for part in parts:
        total = None
        for p in range(2):
            value = scales[p] * jnp.dot(
                acts[p], weights[3 * p + 2][0, :, part], preferred_element_type=jnp.float32
            )
            total = value if total is None else total + value
        total = total.astype(jnp.bfloat16)
        for i, o in enumerate(outs):
            o[:, part] = total[i * rows : (i + 1) * rows]


def stage_kernel(count, *refs):
    sources, targets, sems = refs[:count], refs[count : 2 * count], refs[2 * count]
    copies = [
        pltpu.make_async_copy(a, b, sems.at[i])
        for i, (a, b) in enumerate(zip(sources, targets, strict=True))
    ]
    for c in copies:
        c.start()
    for c in copies:
        c.wait()


def stage(*arrays):
    count = len(arrays)
    return pl.pallas_call(
        functools.partial(stage_kernel, count),
        out_shape=[pltpu.VMEM(a.shape, a.dtype) for a in arrays],
        in_specs=[pl.BlockSpec(memory_space=pltpu.HBM)] * count,
        out_specs=[pl.BlockSpec(memory_space=pltpu.VMEM)] * count,
        scratch_shapes=[pltpu.SemaphoreType.DMA((count,))],
        compiler_params=pltpu.CompilerParams(vmem_limit_bytes=1 << 20),
        cost_estimate=pl.CostEstimate(
            flops=0, bytes_accessed=sum(2 * a.size for a in arrays), transcendentals=0
        ),
        name="stage",
    )(*(pltpu.with_memory_space_constraint(a, pltpu.HBM) for a in arrays))


def run_experts(blocks, masks, weights):
    count = len(blocks)
    rows, packed = blocks[0].shape
    width, hidden = weights[0].shape[1:]
    steps = width // chunk_of(width, 1024)
    operands = [pltpu.with_memory_space_constraint(a, pltpu.VMEM) for a in (*blocks, masks, *weights)]
    return pl.pallas_call(
        functools.partial(expert_kernel, count, steps),
        out_shape=[pltpu.VMEM((rows, width), jnp.bfloat16)] * count,
        in_specs=[pl.BlockSpec(memory_space=pltpu.VMEM)] * len(operands),
        out_specs=[pl.BlockSpec(memory_space=pltpu.VMEM)] * count,
        compiler_params=pltpu.CompilerParams(vmem_limit_bytes=2 * count * rows * packed + (16 << 20)),
        cost_estimate=pl.CostEstimate(
            flops=2 * count * rows * width * hidden * 6,
            bytes_accessed=2 * 6 * width * hidden,
            transcendentals=0,
        ),
        name="experts",
    )(*operands)


def probabilities(queries, latent_cache, lengths):
    score_scale = HEAD_QK ** (-0.5)
    scores = (
        jnp.einsum("rhk,rlk->rhl", queries, latent_cache, preferred_element_type=jnp.float32)
        * score_scale
    )
    positions = jnp.arange(latent_cache.shape[1], dtype=jnp.int32)
    visible = positions[None, None, :] < lengths[:, None, None]
    scores = jnp.where(visible, scores, -1e30)
    row_max = jnp.max(scores, axis=-1, keepdims=True)
    expo = jnp.exp(scores - row_max)
    row_sum = jnp.sum(expo, axis=-1, keepdims=True)
    return (expo / row_sum).astype(jnp.bfloat16)


def attend(probs, latent_cache):
    context = jnp.einsum(
        "rhl,rlk->rhk", probs, latent_cache[:, :, :LAT], preferred_element_type=jnp.float32
    )
    return context.astype(jnp.bfloat16)


def add_all(*terms):
    total = terms[0].astype(jnp.float32)
    for t in terms[1:]:
        total = total + t.astype(jnp.float32)
    return total.astype(jnp.bfloat16)


def body(tokens, routes, route_weight, w_gate, w_up, w_down, queries, latent_cache, lengths):
    nodes, devs = lax.axis_size("node"), lax.axis_size("dev")
    experts_all = nodes * devs // SLICES
    lines = devs // PAIR

    def hop(value, offset):
        return lax.ppermute(value, "dev", [(d, d ^ offset) for d in range(devs)])

    def swap(value):
        return lax.ppermute(value, "node", [(i, i ^ 1) for i in range(nodes)])

    barrier = lax.optimization_barrier
    dev, node = lax.axis_index("dev"), lax.axis_index("node")
    experts_here = jnp.stack([n * devs + dev for n in (node, node ^ 1)]) // SLICES
    extra = -(-3 * experts_all // LANES) * LANES
    column = jnp.arange(extra, dtype=jnp.int32)
    named = jnp.where(column < 3 * experts_all, column % experts_all, -1)
    masks = (named[None, :] == experts_here[:, None]).astype(jnp.float32)
    packed = pack(tokens, routes, route_weight, experts_all)

    w_gate, w_up, packed = barrier((w_gate, w_up, packed))
    w_down, masks = barrier((w_down, masks))
    gate_there, up_there = swap(w_gate), swap(w_up)
    bits = [1 << i for i in reversed(range(lines.bit_length() - 1))]
    gathered, across = {0: packed}, {}
    for bit in bits:
        gathered[bit] = hop(packed, (2 * bit - 1) * PAIR)
    across[0] = hop(packed, 1)
    weights_here = stage(w_gate, w_up, w_down)
    gathered, weights_here, gate_there = barrier((gathered, weights_here, gate_there))
    down_there = swap(w_down)
    into_there = stage(gate_there, up_there)
    for bit in bits[1:]:
        for m in sorted(gathered):
            if m & -m > bit:
                gathered[m ^ bit] = hop(gathered[m], (2 * bit - 1) * PAIR)
    other, far, into_there = barrier((across[0], gathered[lines - 1], into_there))
    gathered[lines - 1] = far
    across[1] = hop(other, PAIR)
    for m in range(2, lines):
        across[m] = hop(gathered[m], 1)
    weights = (*weights_here, *into_there, *stage(down_there))

    rows = tokens.shape[0]
    batch = max(1, CALL_ROWS // (PAIR * rows))
    terms = {}
    for first in range(0, lines, batch):
        cut = [(m, s) for m in range(first, min(lines, first + batch)) for s in range(PAIR)]
        blocks = [(gathered, across)[s][m] for m, s in cut]
        for key, value in zip(cut, run_experts(blocks, masks, weights), strict=True):
            terms[key] = [value]
    probs = probabilities(queries, latent_cache, lengths)

    aside = hop(add_all(*terms.pop((1, 1))), PAIR)
    before = None
    for m in reversed(range(lines)):
        if m == 1:
            continue
        out = add_all(*terms.pop((m, 1)))
        if before is not None:
            out, terms[before, 0][-1] = barrier((out, terms[before, 0][-1]))
        terms[m, 0].append(hop(out, 1))
        before = m
        if m == lines - 1:
            terms[0, 1].append(aside)
        elif m == lines - 2:
            terms[m, 0][-1], terms[0, 1][-1] = barrier((terms[m, 0][-1], terms[0, 1][-1]))
    for bit in reversed(bits):
        before = None
        for m in sorted([m for m, _ in terms if m & bit], reverse=True):
            out = add_all(*terms.pop((m, 0)))
            if before is not None:
                out, terms[before, 0][-1] = barrier((out, terms[before, 0][-1]))
            terms[m ^ bit, 0].append(hop(out, (2 * bit - 1) * PAIR))
            before = m ^ bit
        if bit == 1:
            probs, terms[0, 0][-1] = barrier((probs, terms[0, 0][-1]))
    return add_all(*terms[0, 0]), attend(probs, latent_cache)


def solution(mesh):
    return jax.shard_map(
        body,
        mesh=mesh,
        in_specs=(
            P(("parts", "node", "dev"), None),
            P(("parts", "node", "dev"), None),
            P(("parts", "node", "dev"), None),
            P(("node", "dev"), None, None),
            P(("node", "dev"), None, None),
            P(("node", "dev"), None, None),
            P(("parts", "node", "dev"), None, None),
            P(("parts", "node", "dev"), None, None),
            P(("parts", "node", "dev")),
        ),
        out_specs=(P(("parts", "node", "dev"), None), P(("parts", "node", "dev"), None, None)),
        check_vma=False,
    )
```
